32 devices in a mesh: ctx: 8 (over z, x), head: 2 (over core), grp: 2 (over y).
Axes of the slice: x: 2, y: 2, z: 4, core: 2. Of those that a mesh axis runs over, the one named last changes fastest.
Arguments:
- tokens: bfloat16 [2, 2048, 3072], P('grp', 'ctx', 'head'), may hold values from -6 to 6
- modulation: bfloat16 [2, 3, 3072], P('grp'), may hold values from -3 to 3
- w_qkv: bfloat16 [3072, 3, 512], P(('ctx', 'grp'), None, 'head'), may hold values from -0.09021098 to 0.09021098
- query_gain: float32 [128], replicated, may hold values from 1 to 6
- key_gain: float32 [128], replicated, may hold values from 1 to 6
- w_out: bfloat16 [512, 3072], P('head'), may hold values from -0.25 to 0.25
Outputs:
- branch: bfloat16 [2, 2048, 3072], P('grp', 'ctx', 'head')
The draws below stay inside these ranges and needn't reach their ends.
All inputs are finite; a program needn't handle non-finite values.
Results may differ from the reference program's by a relative error of at most 0.02.
The reference program's roundings to bfloat16 on the way count: a program that leaves them out, or rounds other values in their place, can miss the bound.
Values may be sent and summed in bfloat16 or wider, within the bound.
No kernel may reach another device: no remote copies, remote signals or barrier semaphores. Data moves between devices by JAX's collectives and lax.ppermute only.
A program may use at most 64 MiB of HBM per device.

```python
import math
import jax
import jax.numpy as jnp
from jax import lax

D = 3072
HDIM = 128
HD = 2
HEADS = 4
SEQ = 2048
N_HEAD = 2
N_GRP = 2


def clipped_normal(key, shape, limit):
    return jnp.clip(jax.random.normal(key, shape, jnp.float32), -limit, limit)


def draw_tokens(key, part):
    key = jax.random.fold_in(key, 11)
    base_key = jax.random.fold_in(key, 0)
    states = clipped_normal(base_key, (N_GRP, SEQ, D), 6.0)
    return states.astype(jnp.bfloat16)


def draw_w_qkv(key, part):
    key = jax.random.fold_in(key, 23)
    weight_key = jax.random.fold_in(key, 0)
    weights = clipped_normal(weight_key, (D, 3, HEADS * HDIM), 4.95) * D ** (-0.5)
    return weights.astype(jnp.bfloat16)


def draw_query_gain(key, part):
    key = jax.random.fold_in(key, 37)
    return jnp.exp(jax.random.uniform(key, (HDIM,), jnp.float32, 0.0, math.log(3.0)))


def draw_key_gain(key, part):
    key = jax.random.fold_in(key, 41)
    return jnp.exp(jax.random.uniform(key, (HDIM,), jnp.float32, 0.0, math.log(3.0)))


def block_scale(own_key, extent, shards, least, high):
    level = 1.0
    for dim, blocks in shards:
        draws = jax.random.uniform(jax.random.fold_in(jax.random.fold_in(own_key, 6), dim), (blocks,), jnp.float32, least / len(shards), high / len(shards))
        level = level * jnp.repeat(jnp.exp(draws), extent[dim] // blocks).reshape((-1,) + (1,) * (len(extent) - 1 - dim))
    return level


def centred(own_key, extent, scale, bound, cuts=(), dtype=jnp.bfloat16):
    entries = jax.random.normal(own_key, extent, jnp.float32) * scale
    if len(cuts) > 0:
        entries = block_scale(own_key, extent, cuts, -0.22, 0.18) * entries
    return jnp.clip(entries, min=-bound, max=bound).astype(dtype)


def setup_inputs(seed: int = 0) -> dict:
    streams_of = jax.random.split(jax.random.key(seed), 7)
    tokens = draw_tokens(jax.random.fold_in(streams_of[6], 71), 0)
    modulation = centred(streams_of[1], (N_GRP, 3, D), 0.5, 3.0, ((0, 2),))
    w_qkv = draw_w_qkv(jax.random.fold_in(streams_of[6], 71), 0)
    query_gain = draw_query_gain(jax.random.fold_in(streams_of[6], 71), 0)
    key_gain = draw_key_gain(jax.random.fold_in(streams_of[6], 71), 0)
    w_out = centred(streams_of[5], (HEADS * HDIM, D), (HEADS * HDIM) ** -0.5, 0.25, ((0, 2),))
    return {"tokens": tokens, "modulation": modulation, "w_qkv": w_qkv, "query_gain": query_gain, "key_gain": key_gain, "w_out": w_out}


def norm_heads(values, gain):
    mean_square = lax.optimization_barrier(jnp.mean(values * values, axis=-1, keepdims=True))
    return (values * lax.rsqrt(mean_square + 1e-06) * gain).astype(jnp.bfloat16)

def one_sequence(hidden, modulation, w_qkv, query_gain, key_gain, w_out):
    floats = hidden.astype(jnp.float32)
    center = lax.optimization_barrier(jnp.mean(floats, axis=-1, keepdims=True))
    spread = lax.optimization_barrier(jnp.mean((floats - center) ** 2, axis=-1, keepdims=True))
    normed = (floats - center) * lax.rsqrt(spread + 1e-06)
    mods = modulation.astype(jnp.float32)
    modulated = (normed * (1.0 + mods[1]) + mods[0]).astype(jnp.bfloat16)
    qkv = jnp.dot(modulated, w_qkv.reshape(D, 3 * HEADS * HDIM), preferred_element_type=jnp.float32)
    qkv = qkv.reshape(SEQ, 3, HEADS, HDIM)
    queries = norm_heads(qkv[:, 0], query_gain).transpose(1, 0, 2)
    keys = norm_heads(qkv[:, 1], key_gain).transpose(1, 0, 2)
    values = qkv[:, 2].astype(jnp.bfloat16).transpose(1, 0, 2)

    def head_attention(triple):
        head_q, head_k, head_v = triple
        scores = jnp.dot(head_q, head_k.T, preferred_element_type=jnp.float32) * HDIM ** (-0.5)
        highest = lax.optimization_barrier(jnp.max(scores, axis=-1, keepdims=True))
        weights = jnp.exp(scores - highest)
        totals = lax.optimization_barrier(jnp.sum(weights, axis=-1, keepdims=True))
        mixed = jnp.dot(weights.astype(jnp.bfloat16), head_v, preferred_element_type=jnp.float32)
        return mixed / totals
    attended = lax.map(head_attention, (queries, keys, values))
    attended = attended.transpose(1, 0, 2).reshape(SEQ, HEADS * HDIM).astype(jnp.bfloat16)
    width = HD * HDIM
    projected = jnp.zeros((SEQ, D), jnp.float32)
    for group in range(N_HEAD):
        partial_sum = jnp.dot(attended[:, group * width:(group + 1) * width], w_out[group * width:(group + 1) * width], preferred_element_type=jnp.float32)
        projected = projected + partial_sum.astype(jnp.bfloat16).astype(jnp.float32)
    return (mods[2] * projected).astype(jnp.bfloat16)

def reference(tokens, modulation, w_qkv, query_gain, key_gain, w_out):
    return jnp.stack([one_sequence(tokens[index], modulation[index], w_qkv, query_gain, key_gain, w_out) for index in range(N_GRP)])
```

```python
import functools
import math

import jax
import jax.numpy as jnp
from jax import lax
from jax.experimental import pallas as pl
from jax.experimental.pallas import tpu as pltpu
from jax.sharding import PartitionSpec as P

HDIM = 128
PAIR = 2
VMEM_LIMIT = 40 * 1024 * 1024
VMEM_SPEC = pl.BlockSpec(memory_space=pltpu.VMEM)


def call(kernel, out_shape, scratch=()):
    return lambda *args: pl.pallas_call(
        kernel,
        out_shape=out_shape,
        in_specs=[VMEM_SPEC] * len(args),
        out_specs=jax.tree.map(lambda unused: VMEM_SPEC, out_shape),
        scratch_shapes=list(scratch),
        compiler_params=pltpu.CompilerParams(vmem_limit_bytes=VMEM_LIMIT),
    )(*args)


def swap(value, axes, sizes, flips):
    total = math.prod(sizes)
    perm = []
    for source in range(total):
        rest, target, weight = source, 0, 1
        for size, flip in zip(reversed(sizes), reversed(flips)):
            target += ((rest % size) ^ flip) * weight
            weight *= size
            rest //= size
        perm.append((source, target))
    return lax.ppermute(value, tuple(axes), perm)


def after(value, *others):
    return lax.optimization_barrier((value, others))[0] if others else value


def all_features(piece, n_head):
    return [piece] + [swap(piece, ["head"], [n_head], [j]) for j in range(1, n_head)]


def spread(piece, n_ctx):
    held = {0: piece}
    bit = n_ctx // PAIR // 2
    while bit:
        for far, one in list(held.items()):
            held[far ^ bit] = swap(one, ["ctx"], [n_ctx], [bit * PAIR])
        bit //= 2
    return [held[far] for far in range(n_ctx // PAIR)]


def norm_rows(pieces, mods_ref, out_ref):
    me = lax.axis_index("head")
    rows, width = pieces[0].shape
    total = width * len(pieces)
    step = 16
    places = [
        pl.ds(pl.multiple_of((me ^ j) * width, 128), width) for j in range(len(pieces))
    ]

    def block(i, unused):
        here = pl.ds(pl.multiple_of(i * step, step), step)
        floats = [piece[here, :].astype(jnp.float32) for piece in pieces]
        center = sum(jnp.sum(x, axis=-1, keepdims=True) for x in floats) / total
        floats = [x - center for x in floats]
        spread = sum(jnp.sum(x * x, axis=-1, keepdims=True) for x in floats) / total
        inverse = lax.rsqrt(spread + 1e-06)
        for x, place in zip(floats, places):
            shift = mods_ref[0:1, place].astype(jnp.float32)
            scale = 1.0 + mods_ref[1:2, place].astype(jnp.float32)
            out_ref[here, place] = (x * inverse * scale + shift).astype(jnp.bfloat16)
        return unused

    lax.fori_loop(0, rows // step, block, 0, unroll=4)


def norm_kernel(n_head, *refs):
    norm_rows(refs[:n_head], *refs[n_head:])


def project(tokens_ref, gains, weights, q_ref, kv_ref):
    out = jnp.dot(tokens_ref[...], weights[...], preferred_element_type=jnp.float32)
    for part, gain_ref in enumerate(gains):
        one = out[:, part * HDIM : (part + 1) * HDIM]
        mean_square = jnp.mean(one * one, axis=-1, keepdims=True)
        one = (one * lax.rsqrt(mean_square + 1e-06) * gain_ref[...]).astype(jnp.bfloat16)
        if part == 0:
            q_ref[...] = one
        else:
            kv_ref[:, :HDIM] = one
    kv_ref[:, HDIM:] = out[:, 2 * HDIM :].astype(jnp.bfloat16)


def first_qkv_kernel(places, n_grp, *refs):
    tokens_ref, qgain_ref, kgain_ref = refs[:3]
    chunks, (q_ref, kv_ref, weights) = refs[3:-3], refs[-3:]
    t = lax.axis_index("ctx")
    g = lax.axis_index("grp")
    rows = chunks[0].shape[0]
    for (far, near, fg), chunk in zip(places, chunks):
        owner = t ^ (far * PAIR + near)
        start = pl.multiple_of((owner * n_grp + (g ^ fg)) * rows, 16)
        weights[pl.ds(start, rows), :] = chunk[...]
    project(tokens_ref, (qgain_ref, kgain_ref), weights, q_ref, kv_ref)


def norm_qkv_kernel(n_head, *refs):
    pieces, (mods_ref, qgain_ref, kgain_ref, weights, q_ref, kv_ref, normed) = (
        refs[:n_head],
        refs[n_head:],
    )
    norm_rows(pieces, mods_ref, normed)
    project(normed, (qgain_ref, kgain_ref), weights, q_ref, kv_ref)


def attend_kernel(count, *refs):
    q_refs, pieces, out_refs = refs[:PAIR], refs[PAIR : PAIR + count], refs[PAIR + count :]
    step = 128
    factor = HDIM ** (-0.5) * math.log2(math.e)
    dims = (((1,), (1,)), ((), ()))
    for q_ref, out_ref in zip(q_refs, out_refs):
        for i in range(q_ref.shape[0] // step):
            here = slice(i * step, (i + 1) * step)
            query = q_ref[here, :]
            scores = [
                lax.dot_general(query, piece[:, :HDIM], dims, preferred_element_type=jnp.float32)
                for piece in pieces
            ]
            highest = functools.reduce(
                jnp.maximum, [jnp.max(s, axis=-1, keepdims=True) for s in scores]
            )
            total = jnp.zeros((step, 1), jnp.float32)
            mixed = jnp.zeros((step, HDIM), jnp.float32)
            for s, piece in zip(scores, pieces):
                weights = jnp.exp2((s - highest) * factor)
                total = total + jnp.sum(weights, axis=-1, keepdims=True)
                mixed = mixed + jnp.dot(
                    weights.astype(jnp.bfloat16),
                    piece[:, HDIM:],
                    preferred_element_type=jnp.float32,
                )
            out_ref[here, :] = (mixed / total).astype(jnp.bfloat16)


def out_kernel(n_head, *refs):
    heads = refs[: PAIR * n_head]
    w_refs = refs[PAIR * n_head : (PAIR + 1) * n_head]
    gate_ref, out_ref, att = refs[(PAIR + 1) * n_head :]
    c = lax.axis_index("head")
    p = lax.axis_index("ctx") % PAIR
    width = out_ref.shape[1]
    mine = pl.ds(pl.multiple_of(c * width, 128), width)
    projected = None
    for j in range(n_head):
        for a in range(PAIR):
            where = pl.ds(pl.multiple_of((p ^ a) * HDIM, HDIM), HDIM)
            att[j, :, where] = heads[j * PAIR + a][...]
        w_rows = w_refs[j][...] if j else w_refs[j][:, mine]
        partial = jnp.dot(att[j], w_rows, preferred_element_type=jnp.float32)
        partial = partial.astype(jnp.bfloat16).astype(jnp.float32)
        projected = partial if projected is None else projected + partial
    gate = gate_ref[2:3, mine].astype(jnp.float32)
    out_ref[...] = (gate * projected).astype(jnp.bfloat16)


def body(sizes, tokens, modulation, w_qkv, query_gain, key_gain, w_out):
    n_ctx, n_head, n_grp = sizes["ctx"], sizes["head"], sizes["grp"]
    t, c = lax.axis_index("ctx"), lax.axis_index("head")
    p = t % PAIR
    tokens, mods = tokens[0], modulation[0]
    count, width = tokens.shape
    rows = w_qkv.shape[0]

    far_count = n_ctx // PAIR
    mine = lax.dynamic_slice_in_dim(w_qkv, p * HDIM, HDIM, 2).reshape(rows, 3 * HDIM)
    given = lax.dynamic_slice_in_dim(w_qkv, (1 - p) * HDIM, HDIM, 2).reshape(rows, 3 * HDIM)
    other = swap(given, ["ctx"], [n_ctx], [1])
    wide = jax.ShapeDtypeStruct((count, width * n_head), jnp.bfloat16)
    own_normed = call(functools.partial(norm_kernel, n_head), wide)(
        *all_features(tokens, n_head), mods
    )

    rows_out = after(w_out, own_normed)
    blocks = [
        lax.dynamic_slice_in_dim(rows_out, (c ^ j) * width, width, 1) for j in range(1, n_head)
    ]
    outs = [swap(block, ["head"], [n_head], [j]) for j, block in enumerate(blocks, 1)]

    chunks, places = [], []
    held = [spread(mine, n_ctx), spread(other, n_ctx)]
    sent = []
    for far in range(far_count):
        for near in range(PAIR):
            piece = held[near][far]
            if len(sent) == 3:
                sent[1] += (own_normed, *blocks)
            if len(sent) >= 2:
                piece = after(piece, *sent[-2])
            if 0 < far < far_count - 1:
                piece = after(piece, held[near][far + 1])
            got = [swap(piece, ["grp"], [n_grp], [fg]) for fg in range(1, n_grp)]
            sent.append(tuple(got))
            for fg, chunk in enumerate([held[near][far]] + got):
                chunks.append(chunk)
                places.append((far, near, fg))
    first = (other, held[0][far_count // 2], held[0][1], *sent[0])
    neighbour = swap(after(tokens, *first), ["ctx"], [n_ctx], [1])
    neighbour = after(neighbour, *sent[-4], *sent[-3])

    piece_shape = jax.ShapeDtypeStruct((count, HDIM), jnp.bfloat16)
    pair_shape = jax.ShapeDtypeStruct((count, 2 * HDIM), jnp.bfloat16)
    gains = (query_gain[None], key_gain[None])
    own_queries, own_kv, weights = call(
        functools.partial(first_qkv_kernel, places, n_grp),
        (
            piece_shape,
            pair_shape,
            jax.ShapeDtypeStruct((rows * len(places), 3 * HDIM), jnp.bfloat16),
        ),
    )(own_normed, *gains, *chunks)
    other_queries, other_kv = call(
        functools.partial(norm_qkv_kernel, n_head),
        (piece_shape, pair_shape),
        [pltpu.VMEM(wide.shape, jnp.bfloat16)],
    )(*all_features(neighbour, n_head), mods, *gains, weights)

    gathered = spread(own_kv, n_ctx) + spread(other_kv, n_ctx)
    att_own, att_other = call(
        functools.partial(attend_kernel, len(gathered)), (piece_shape, piece_shape)
    )(own_queries, other_queries, *gathered)

    heads = []
    for j in range(n_head):
        for a in range(PAIR):
            piece = att_other if a else att_own
            if j or a:
                piece = swap(piece, ["ctx", "head"], [n_ctx, n_head], [a, j])
            heads.append(piece)
    branch = call(
        functools.partial(out_kernel, n_head),
        jax.ShapeDtypeStruct((count, width), jnp.bfloat16),
        [pltpu.VMEM((n_head, count, PAIR * HDIM), jnp.bfloat16)],
    )(*heads, w_out, *outs, mods)
    return branch[None]


def solution(mesh):
    in_specs = (
        P("grp", "ctx", "head"),
        P("grp", None, None),
        P(("ctx", "grp"), None, "head"),
        P(),
        P(),
        P("head", None),
    )
    out_specs = P("grp", "ctx", "head")
    return jax.shard_map(
        functools.partial(body, dict(mesh.shape)),
        mesh=mesh,
        in_specs=in_specs,
        out_specs=out_specs,
        check_vma=False,
    )
```

```python
import functools
import math

import jax
import jax.numpy as jnp
from jax import lax
from jax.experimental import pallas as pl
from jax.experimental.pallas import tpu as pltpu
from jax.sharding import PartitionSpec as P

HDIM = 128
PAIR = 2
VMEM_LIMIT = 40 * 1024 * 1024
VMEM_SPEC = pl.BlockSpec(memory_space=pltpu.VMEM)


def call(kernel, out_shape, scratch=()):
    return lambda *args: pl.pallas_call(
        kernel,
        out_shape=out_shape,
        in_specs=[VMEM_SPEC] * len(args),
        out_specs=jax.tree.map(lambda unused: VMEM_SPEC, out_shape),
        scratch_shapes=list(scratch),
        compiler_params=pltpu.CompilerParams(vmem_limit_bytes=VMEM_LIMIT),
    )(*args)


def swap(value, axes, sizes, flips):
    total = math.prod(sizes)
    perm = []
    for source in range(total):
        rest, target, weight = source, 0, 1
        for size, flip in zip(reversed(sizes), reversed(flips)):
            target += ((rest % size) ^ flip) * weight
            weight *= size
            rest //= size
        perm.append((source, target))
    return lax.ppermute(value, tuple(axes), perm)


def after(value, *others):
    return lax.optimization_barrier((value, others))[0] if others else value


def all_features(piece, n_head):
    return [piece] + [swap(piece, ["head"], [n_head], [j]) for j in range(1, n_head)]


def tree(count):
    known, found = [0], []
    bit = count // 2
    while bit:
        found += [(far ^ bit, far) for far in known]
        known += [far ^ bit for far in known]
        bit //= 2
    return found


def spread(piece, n_ctx):
    held = {0: piece}
    for far, source in tree(n_ctx // PAIR):
        held[far] = swap(held[source], ["ctx"], [n_ctx], [(far ^ source) * PAIR])
    return [held[far] for far in range(n_ctx // PAIR)]


def norm_rows(pieces, mods_ref, out_ref):
    me = lax.axis_index("head")
    rows, width = pieces[0].shape
    total = width * len(pieces)
    step = 16
    places = [
        pl.ds(pl.multiple_of((me ^ j) * width, 128), width) for j in range(len(pieces))
    ]

    def block(i, unused):
        here = pl.ds(pl.multiple_of(i * step, step), step)
        floats = [piece[here, :].astype(jnp.float32) for piece in pieces]
        center = sum(jnp.sum(x, axis=-1, keepdims=True) for x in floats) / total
        floats = [x - center for x in floats]
        spread = sum(jnp.sum(x * x, axis=-1, keepdims=True) for x in floats) / total
        inverse = lax.rsqrt(spread + 1e-06)
        for x, place in zip(floats, places):
            shift = mods_ref[0:1, place].astype(jnp.float32)
            scale = 1.0 + mods_ref[1:2, place].astype(jnp.float32)
            out_ref[here, place] = (x * inverse * scale + shift).astype(jnp.bfloat16)
        return unused

    lax.fori_loop(0, rows // step, block, 0, unroll=4)


def norm_kernel(n_head, *refs):
    norm_rows(refs[:n_head], *refs[n_head:])


def project(tokens_ref, gains, weights, q_ref, kv_ref):
    out = jnp.dot(tokens_ref[...], weights[...], preferred_element_type=jnp.float32)
    for part, gain_ref in enumerate(gains):
        one = out[:, part * HDIM : (part + 1) * HDIM]
        mean_square = jnp.mean(one * one, axis=-1, keepdims=True)
        one = (one * lax.rsqrt(mean_square + 1e-06) * gain_ref[...]).astype(jnp.bfloat16)
        if part == 0:
            q_ref[...] = one
        else:
            kv_ref[:, :HDIM] = one
    kv_ref[:, HDIM:] = out[:, 2 * HDIM :].astype(jnp.bfloat16)


def qkv_kernel(places, n_grp, *refs):
    tokens_refs, gains = refs[:PAIR], refs[PAIR : PAIR + 2]
    chunks, out_refs, weights = refs[PAIR + 2 : -5], refs[-5:-1], refs[-1]
    t = lax.axis_index("ctx")
    g = lax.axis_index("grp")
    rows = chunks[0].shape[0]
    for (far, near, fg), chunk in zip(places, chunks):
        owner = t ^ (far * PAIR + near)
        start = pl.multiple_of((owner * n_grp + (g ^ fg)) * rows, 16)
        weights[pl.ds(start, rows), :] = chunk[...]
    for i, tokens_ref in enumerate(tokens_refs):
        project(tokens_ref, gains, weights, out_refs[2 * i], out_refs[2 * i + 1])


def attend_kernel(count, *refs):
    q_refs, pieces, out_refs = refs[:PAIR], refs[PAIR : PAIR + count], refs[PAIR + count :]
    step = 128
    factor = HDIM ** (-0.5) * math.log2(math.e)
    dims = (((1,), (1,)), ((), ()))
    for q_ref, out_ref in zip(q_refs, out_refs):
        for i in range(q_ref.shape[0] // step):
            here = slice(i * step, (i + 1) * step)
            query = q_ref[here, :]
            scores = [
                lax.dot_general(query, piece[:, :HDIM], dims, preferred_element_type=jnp.float32)
                for piece in pieces
            ]
            highest = functools.reduce(
                jnp.maximum, [jnp.max(s, axis=-1, keepdims=True) for s in scores]
            )
            total = jnp.zeros((step, 1), jnp.float32)
            mixed = jnp.zeros((step, HDIM), jnp.float32)
            for s, piece in zip(scores, pieces):
                weights = jnp.exp2((s - highest) * factor)
                total = total + jnp.sum(weights, axis=-1, keepdims=True)
                mixed = mixed + jnp.dot(
                    weights.astype(jnp.bfloat16),
                    piece[:, HDIM:],
                    preferred_element_type=jnp.float32,
                )
            out_ref[here, :] = (mixed / total).astype(jnp.bfloat16)


def out_kernel(n_head, *refs):
    heads = refs[: PAIR * n_head]
    w_refs = refs[PAIR * n_head : (PAIR + 1) * n_head]
    gate_ref, out_ref, att = refs[(PAIR + 1) * n_head :]
    c = lax.axis_index("head")
    p = lax.axis_index("ctx") % PAIR
    width = out_ref.shape[1]
    mine = pl.ds(pl.multiple_of(c * width, 128), width)
    projected = None
    for j in range(n_head):
        for a in range(PAIR):
            where = pl.ds(pl.multiple_of((p ^ a) * HDIM, HDIM), HDIM)
            att[j, :, where] = heads[j * PAIR + a][...]
        w_rows = w_refs[j][...] if j else w_refs[j][:, mine]
        partial = jnp.dot(att[j], w_rows, preferred_element_type=jnp.float32)
        partial = partial.astype(jnp.bfloat16).astype(jnp.float32)
        projected = partial if projected is None else projected + partial
    gate = gate_ref[2:3, mine].astype(jnp.float32)
    out_ref[...] = (gate * projected).astype(jnp.bfloat16)


def body(sizes, tokens, modulation, w_qkv, query_gain, key_gain, w_out):
    n_ctx, n_head, n_grp = sizes["ctx"], sizes["head"], sizes["grp"]
    t, c = lax.axis_index("ctx"), lax.axis_index("head")
    p = t % PAIR
    tokens, mods = tokens[0], modulation[0]
    count, width = tokens.shape
    rows = w_qkv.shape[0]

    far_count = n_ctx // PAIR
    mine = lax.dynamic_slice_in_dim(w_qkv, p * HDIM, HDIM, 2).reshape(rows, 3 * HDIM)
    given = lax.dynamic_slice_in_dim(w_qkv, (1 - p) * HDIM, HDIM, 2).reshape(rows, 3 * HDIM)
    other = swap(given, ["ctx"], [n_ctx], [1])
    wide = jax.ShapeDtypeStruct((count, width * n_head), jnp.bfloat16)
    own_normed = call(functools.partial(norm_kernel, n_head), wide)(
        *all_features(tokens, n_head), mods
    )

    rows_out = after(w_out, own_normed)
    blocks = [
        lax.dynamic_slice_in_dim(rows_out, (c ^ j) * width, width, 1) for j in range(1, n_head)
    ]
    outs = [swap(block, ["head"], [n_head], [j]) for j, block in enumerate(blocks, 1)]

    found = tree(far_count)
    ready = [0] + [far for far, unused in found]
    plan = [found[0], (0, None)]
    plan = [(near, *step) for near in range(PAIR) for step in plan]
    plan += [(near, *step) for step in found[1:2] for near in range(PAIR)]
    for i in range(2, len(found)):
        for near in range(PAIR):
            plan += [(near, *found[i]), (near, ready[i - 1], None)]
    plan += [(near, far, None) for far in ready[-2:] for near in range(PAIR)]
    held = [{0: mine}, {0: other}]
    chunks, places, results = [], [], [(other,)]
    for near, far, source in plan:
        piece = held[near][far if source is None else source]
        if len(results) >= 5:
            piece = after(piece, *sum(results[:-4], ()))
        if source is None:
            got = [swap(piece, ["grp"], [n_grp], [fg]) for fg in range(1, n_grp)]
            for fg, chunk in enumerate([held[near][far]] + got):
                chunks.append(chunk)
                places.append((far, near, fg))
        else:
            got = [swap(piece, ["ctx"], [n_ctx], [(far ^ source) * PAIR])]
            held[near][far] = got[0]
        results.append(tuple(got))
        if len(results) == len(plan) // 2 - 1:
            results[-1] += (own_normed, *blocks)
    neighbour = swap(after(tokens, *results[0], *results[2]), ["ctx"], [n_ctx], [1])
    neighbour = after(neighbour, *sum(results[:-1], ()))
    other_normed = call(functools.partial(norm_kernel, n_head), wide)(
        *all_features(neighbour, n_head), mods
    )

    piece_shape = jax.ShapeDtypeStruct((count, HDIM), jnp.bfloat16)
    pair_shape = jax.ShapeDtypeStruct((count, 2 * HDIM), jnp.bfloat16)
    gains = (query_gain[None], key_gain[None])
    own_queries, own_kv, other_queries, other_kv = call(
        functools.partial(qkv_kernel, places, n_grp),
        (piece_shape, pair_shape) * PAIR,
        [pltpu.VMEM((rows * len(places), 3 * HDIM), jnp.bfloat16)],
    )(own_normed, other_normed, *gains, *chunks)
    gathered = spread(own_kv, n_ctx) + spread(other_kv, n_ctx)
    att_own, att_other = call(
        functools.partial(attend_kernel, len(gathered)), (piece_shape, piece_shape)
    )(own_queries, other_queries, *gathered)

    heads = []
    for j in range(n_head):
        for a in range(PAIR):
            piece = att_other if a else att_own
            if j or a:
                piece = swap(piece, ["ctx", "head"], [n_ctx, n_head], [a, j])
            heads.append(piece)
    branch = call(
        functools.partial(out_kernel, n_head),
        jax.ShapeDtypeStruct((count, width), jnp.bfloat16),
        [pltpu.VMEM((n_head, count, PAIR * HDIM), jnp.bfloat16)],
    )(*heads, w_out, *outs, mods)
    return branch[None]


def solution(mesh):
    in_specs = (
        P("grp", "ctx", "head"),
        P("grp", None, None),
        P(("ctx", "grp"), None, "head"),
        P(),
        P(),
        P("head", None),
    )
    out_specs = P("grp", "ctx", "head")
    return jax.shard_map(
        functools.partial(body, dict(mesh.shape)),
        mesh=mesh,
        in_specs=in_specs,
        out_specs=out_specs,
        check_vma=False,
    )
```

```python
import functools
import math

import jax
import jax.numpy as jnp
from jax import lax
from jax.experimental import pallas as pl
from jax.experimental.pallas import tpu as pltpu
from jax.sharding import PartitionSpec as P

HDIM = 128
PAIR = 2
VMEM_LIMIT = 40 * 1024 * 1024
VMEM_SPEC = pl.BlockSpec(memory_space=pltpu.VMEM)


def call(kernel, out_shape, scratch=()):
    return lambda *args: pl.pallas_call(
        kernel,
        out_shape=out_shape,
        in_specs=[VMEM_SPEC] * len(args),
        out_specs=jax.tree.map(lambda unused: VMEM_SPEC, out_shape),
        scratch_shapes=list(scratch),
        compiler_params=pltpu.CompilerParams(vmem_limit_bytes=VMEM_LIMIT),
    )(*args)


def swap(value, axes, sizes, flips):
    total = math.prod(sizes)
    perm = []
    for source in range(total):
        rest, target, weight = source, 0, 1
        for size, flip in zip(reversed(sizes), reversed(flips)):
            target += ((rest % size) ^ flip) * weight
            weight *= size
            rest //= size
        perm.append((source, target))
    return lax.ppermute(value, tuple(axes), perm)


def after(value, *others):
    return lax.optimization_barrier((value, others))[0] if others else value


def all_features(piece, n_head):
    return [piece] + [swap(piece, ["head"], [n_head], [j]) for j in range(1, n_head)]


def tree(count):
    known, found = [0], []
    bit = count // 2
    while bit:
        found += [(far ^ bit, far) for far in known]
        known += [far ^ bit for far in known]
        bit //= 2
    return found


def spread(piece, n_ctx):
    held = {0: piece}
    for far, source in tree(n_ctx // PAIR):
        held[far] = swap(held[source], ["ctx"], [n_ctx], [(far ^ source) * PAIR])
    return [held[far] for far in range(n_ctx // PAIR)]


def norm_rows(pieces, mods_ref, out_ref):
    me = lax.axis_index("head")
    rows, width = pieces[0].shape
    total = width * len(pieces)
    step = 16
    places = [
        pl.ds(pl.multiple_of((me ^ j) * width, 128), width) for j in range(len(pieces))
    ]

    def block(i, unused):
        here = pl.ds(pl.multiple_of(i * step, step), step)
        floats = [piece[here, :].astype(jnp.float32) for piece in pieces]
        center = sum(jnp.sum(x, axis=-1, keepdims=True) for x in floats) / total
        floats = [x - center for x in floats]
        spread = sum(jnp.sum(x * x, axis=-1, keepdims=True) for x in floats) / total
        inverse = lax.rsqrt(spread + 1e-06)
        for x, place in zip(floats, places):
            shift = mods_ref[0:1, place].astype(jnp.float32)
            scale = 1.0 + mods_ref[1:2, place].astype(jnp.float32)
            out_ref[here, place] = (x * inverse * scale + shift).astype(jnp.bfloat16)
        return unused

    lax.fori_loop(0, rows // step, block, 0, unroll=4)


def norm_kernel(n_head, *refs):
    norm_rows(refs[:n_head], *refs[n_head:])


def project(tokens_ref, gains, weights, q_ref, kv_ref):
    out = jnp.dot(tokens_ref[...], weights[...], preferred_element_type=jnp.float32)
    for part, gain_ref in enumerate(gains):
        one = out[:, part * HDIM : (part + 1) * HDIM]
        mean_square = jnp.mean(one * one, axis=-1, keepdims=True)
        one = (one * lax.rsqrt(mean_square + 1e-06) * gain_ref[...]).astype(jnp.bfloat16)
        if part == 0:
            q_ref[...] = one
        else:
            kv_ref[:, :HDIM] = one
    kv_ref[:, HDIM:] = out[:, 2 * HDIM :].astype(jnp.bfloat16)


def qkv_kernel(places, n_grp, *refs):
    tokens_refs, gains = refs[:PAIR], refs[PAIR : PAIR + 2]
    chunks, out_refs, weights = refs[PAIR + 2 : -5], refs[-5:-1], refs[-1]
    t = lax.axis_index("ctx")
    g = lax.axis_index("grp")
    rows = chunks[0].shape[0] // PAIR
    for (far, fg), chunk in zip(places, chunks):
        for near in range(PAIR):
            owner = t ^ (far * PAIR + near)
            start = pl.multiple_of((owner * n_grp + (g ^ fg)) * rows, 16)
            weights[pl.ds(start, rows), :] = chunk[near * rows : (near + 1) * rows, :]
    for i, tokens_ref in enumerate(tokens_refs):
        project(tokens_ref, gains, weights, out_refs[2 * i], out_refs[2 * i + 1])


def attend_kernel(count, *refs):
    q_refs, pieces, out_refs = refs[:PAIR], refs[PAIR : PAIR + count], refs[PAIR + count :]
    step = 128
    factor = HDIM ** (-0.5) * math.log2(math.e)
    dims = (((1,), (1,)), ((), ()))
    for q_ref, out_ref in zip(q_refs, out_refs):
        for i in range(q_ref.shape[0] // step):
            here = slice(i * step, (i + 1) * step)
            query = q_ref[here, :]
            scores = [
                lax.dot_general(query, piece[:, :HDIM], dims, preferred_element_type=jnp.float32)
                for piece in pieces
            ]
            highest = functools.reduce(
                jnp.maximum, [jnp.max(s, axis=-1, keepdims=True) for s in scores]
            )
            total = jnp.zeros((step, 1), jnp.float32)
            mixed = jnp.zeros((step, HDIM), jnp.float32)
            for s, piece in zip(scores, pieces):
                weights = jnp.exp2((s - highest) * factor)
                total = total + jnp.sum(weights, axis=-1, keepdims=True)
                mixed = mixed + jnp.dot(
                    weights.astype(jnp.bfloat16),
                    piece[:, HDIM:],
                    preferred_element_type=jnp.float32,
                )
            out_ref[here, :] = (mixed / total).astype(jnp.bfloat16)


def out_kernel(n_head, *refs):
    heads = refs[: PAIR * n_head]
    w_refs = refs[PAIR * n_head : (PAIR + 1) * n_head]
    gate_ref, out_ref, att = refs[(PAIR + 1) * n_head :]
    c = lax.axis_index("head")
    p = lax.axis_index("ctx") % PAIR
    width = out_ref.shape[1]
    mine = pl.ds(pl.multiple_of(c * width, 128), width)
    projected = None
    for j in range(n_head):
        for a in range(PAIR):
            where = pl.ds(pl.multiple_of((p ^ a) * HDIM, HDIM), HDIM)
            att[j, :, where] = heads[j * PAIR + a][...]
        w_rows = w_refs[j][...] if j else w_refs[j][:, mine]
        partial = jnp.dot(att[j], w_rows, preferred_element_type=jnp.float32)
        partial = partial.astype(jnp.bfloat16).astype(jnp.float32)
        projected = partial if projected is None else projected + partial
    gate = gate_ref[2:3, mine].astype(jnp.float32)
    out_ref[...] = (gate * projected).astype(jnp.bfloat16)


def body(sizes, tokens, modulation, w_qkv, query_gain, key_gain, w_out):
    n_ctx, n_head, n_grp = sizes["ctx"], sizes["head"], sizes["grp"]
    t, c = lax.axis_index("ctx"), lax.axis_index("head")
    p = t % PAIR
    tokens, mods = tokens[0], modulation[0]
    count, width = tokens.shape
    rows = w_qkv.shape[0]

    far_count = n_ctx // PAIR
    mine = lax.dynamic_slice_in_dim(w_qkv, p * HDIM, HDIM, 2).reshape(rows, 3 * HDIM)
    given = lax.dynamic_slice_in_dim(w_qkv, (1 - p) * HDIM, HDIM, 2).reshape(rows, 3 * HDIM)
    other = swap(given, ["ctx"], [n_ctx], [1])
    wide = jax.ShapeDtypeStruct((count, width * n_head), jnp.bfloat16)
    own_normed = call(functools.partial(norm_kernel, n_head), wide)(
        *all_features(tokens, n_head), mods
    )

    rows_out = after(w_out, own_normed)
    blocks = [
        lax.dynamic_slice_in_dim(rows_out, (c ^ j) * width, width, 1) for j in range(1, n_head)
    ]
    outs = [swap(block, ["head"], [n_head], [j]) for j, block in enumerate(blocks, 1)]

    found = tree(far_count)
    top = found[0][0]
    halves = [swap(piece, ["ctx"], [n_ctx], [top * PAIR]) for piece in (mine, other)]
    held = {0: jnp.concatenate([mine, other]), top: jnp.concatenate(halves)}
    for far, source in found[1:]:
        held[far] = swap(held[source], ["ctx"], [n_ctx], [(far ^ source) * PAIR])
    chunks, places, sent = [], [], []
    order = sorted(range(far_count), key=lambda far: (far.bit_count(), far))
    for i, far in enumerate(order):
        waits = sent[i - 2] if i >= 2 else ()
        if i == 2:
            waits += (own_normed, *blocks, held[order[1]])
        piece = after(held[far], *waits)
        got = [swap(piece, ["grp"], [n_grp], [fg]) for fg in range(1, n_grp)]
        sent.append(tuple(got))
        for fg, chunk in enumerate([held[far]] + got):
            chunks.append(chunk)
            places.append((far, fg))
    neighbour = swap(after(tokens, other, halves[0]), ["ctx"], [n_ctx], [1])
    neighbour = after(neighbour, *sent[-3], *sent[-2], held[order[-1]])
    other_normed = call(functools.partial(norm_kernel, n_head), wide)(
        *all_features(neighbour, n_head), mods
    )

    piece_shape = jax.ShapeDtypeStruct((count, HDIM), jnp.bfloat16)
    pair_shape = jax.ShapeDtypeStruct((count, 2 * HDIM), jnp.bfloat16)
    gains = (query_gain[None], key_gain[None])
    own_queries, own_kv, other_queries, other_kv = call(
        functools.partial(qkv_kernel, places, n_grp),
        (piece_shape, pair_shape) * PAIR,
        [pltpu.VMEM((PAIR * rows * len(places), 3 * HDIM), jnp.bfloat16)],
    )(own_normed, other_normed, *gains, *chunks)
    gathered = spread(own_kv, n_ctx) + spread(other_kv, n_ctx)
    att_own, att_other = call(
        functools.partial(attend_kernel, len(gathered)), (piece_shape, piece_shape)
    )(own_queries, other_queries, *gathered)

    heads = []
    for j in range(n_head):
        for a in range(PAIR):
            piece = att_other if a else att_own
            if j or a:
                piece = swap(piece, ["ctx", "head"], [n_ctx, n_head], [a, j])
            heads.append(piece)
    branch = call(
        functools.partial(out_kernel, n_head),
        jax.ShapeDtypeStruct((count, width), jnp.bfloat16),
        [pltpu.VMEM((n_head, count, PAIR * HDIM), jnp.bfloat16)],
    )(*heads, w_out, *outs, mods)
    return branch[None]


def solution(mesh):
    in_specs = (
        P("grp", "ctx", "head"),
        P("grp", None, None),
        P(("ctx", "grp"), None, "head"),
        P(),
        P(),
        P("head", None),
    )
    out_specs = P("grp", "ctx", "head")
    return jax.shard_map(
        functools.partial(body, dict(mesh.shape)),
        mesh=mesh,
        in_specs=in_specs,
        out_specs=out_specs,
        check_vma=False,
    )
```
